256 devices in a mesh: src: 8 (over z_lo, x), space: 32 (over y, z_hi, core).
Axes of the slice: x: 4, y: 4, z: 8 (z_hi: 4, z_lo: 2; z = z_hi * 2 + z_lo), core: 2. Of those that a mesh axis runs over, the one named last changes fastest.
Arguments:
- fwd_current: float32 [8, 3, 256, 64, 128], P('src', None, 'space'), may hold values from -6 to 6
- adj_current: float32 [8, 3, 256, 64, 128], P('src', None, 'space'), may hold values from -6 to 6
- inv_eps: float32 [256, 64, 128], P('space'), may hold values from 0.25 to 1
- wavelength: int32 [8], P('src'), may hold values from 0 to 15
- footprint: int32 [256, 64], P('space', 'src'), may hold values from 0 to 4095, as said below
Outputs:
- design_grad: float32 [4096, 128], P(('src', 'space'))
The draws below stay inside these ranges and needn't reach their ends.
Inputs may be any that keep to these rules, and one draw needn't show every extreme that they name: `footprint`: A column (x, y) whose y lies in the i-th block of 8 cells names a pixel of the pixel blocks i * 32 to (i + 1) * 32 - 1, a pixel block being 16 consecutive pixels. Among the 64 columns of one slab of 8 cells in x and one block in y, at most 4 name pixels of any one pixel block; in each group i one pixel block receives exactly 4 columns from every slab.
All inputs are finite; a program needn't handle non-finite values.
Results may differ from the reference program's by a relative error of at most 0.0003.
Values sent between devices are 32-bit elements; how exact they have to be, the bound alone decides.
No kernel may reach another device: no remote copies, remote signals or barrier semaphores. Data moves between devices by JAX's collectives and lax.ppermute only.
A program may use at most 64 MiB of HBM per device.

```python
import math
import jax
import jax.numpy as jnp
from jax import lax

CX = 8
NY = 64
NZ = 128
ITERS = 4
PIX_DEV = 16
NX = 256
SOURCES = 8
GROUPS = 8
OWNERS = 32
YSHARE = 8
ROWS = 64
CAP = 4
PIX = 4096


def draw_footprint(key, part):
    slots = OWNERS * CAP
    heavy = jax.random.randint(jax.random.fold_in(key, 1), (GROUPS,), 0, OWNERS)

    def one_block(block_key, group):
        first, second, third = jax.random.split(block_key, 3)
        shuffled = jax.random.permutation(first, slots)
        owner = shuffled // CAP
        score = jnp.where(owner == heavy[group], 0, 1) * slots + jnp.arange(slots)
        order = jnp.argsort(score)
        chosen = shuffled[order][:ROWS]
        chosen = chosen[jax.random.permutation(second, ROWS)]
        within = jax.random.randint(third, (ROWS,), 0, PIX_DEV)
        return ((group * OWNERS + chosen // CAP) * PIX_DEV + within).astype(jnp.int32)
    block_keys = jax.random.split(jax.random.fold_in(key, 2), OWNERS * GROUPS)
    group_ids = jnp.tile(jnp.arange(GROUPS), OWNERS)
    pixels = jax.vmap(one_block)(block_keys, group_ids)
    pixels = pixels.reshape(OWNERS, GROUPS, CX, YSHARE).transpose(0, 2, 1, 3)
    return pixels.reshape(NX, NY).astype(jnp.int32)


def set_ends(drawn, stream_key, least, high):
    longest = drawn.shape.index(max(drawn.shape))
    spots = []
    for shift in (0, 1):
        where = [jax.random.randint(jax.random.fold_in(stream_key, axis), (), 0, length) for axis, length in enumerate(drawn.shape)]
        where[longest] = (where[longest] + shift) % drawn.shape[longest]
        spots.append(tuple(where))
    return drawn.at[spots[0]].set(least).at[spots[1]].set(high)


def levels(rng, shape, pieces, smallest, largest):
    gain, own = 1.0, jax.random.fold_in(rng, 6)
    for position, blocks in pieces:
        steps = jnp.exp(jax.random.uniform(jax.random.fold_in(own, position), (blocks,), jnp.float32, smallest / len(pieces), largest / len(pieces)))
        gain = gain * jnp.repeat(steps, shape[position] // blocks).reshape([-1 if axis == position else 1 for axis in range(len(shape))])
    return gain


def noise(own_key, extent, deviation, most, cuts=(), held_as=jnp.bfloat16):
    drawn = deviation * jax.random.normal(own_key, extent, jnp.float32)
    if cuts:
        drawn = drawn * levels(own_key, extent, cuts, -0.22, 0.18)
    return jnp.clip(drawn, -most, most).astype(held_as)


def setup_inputs(seed: int = 0) -> dict:
    key_list = jax.random.split(jax.random.key(seed), 6)
    return {
        "fwd_current": noise(key_list[0], (SOURCES, 3, NX, NY, NZ), 1.0, 6.0, ((0, 8), (2, 32)), jnp.float32),
        "adj_current": noise(key_list[1], (SOURCES, 3, NX, NY, NZ), 1.0, 6.0, ((0, 8), (2, 32)), jnp.float32),
        "inv_eps": jnp.clip(jnp.exp(math.log(1.0) - 1.3862944 * jax.random.uniform(key_list[2], (NX, NY, NZ), jnp.float32) ** levels(key_list[2], (NX, NY, NZ), ((0, 32),), -0.2, 0.2)), 0.25, 1.0),
        "wavelength": set_ends(jax.random.randint(key_list[3], (SOURCES,), 0, 16), jax.random.fold_in(key_list[3], 1), 0, 15).astype(jnp.int32),
        "footprint": draw_footprint(jax.random.fold_in(key_list[5], 71), 0),
    }


COURANT = 0.5


def diff_fwd(field, axis):
    if axis == 0:
        ahead = jnp.concatenate([field[1:], jnp.zeros_like(field[:1])], axis=0)
    else:
        ahead = jnp.roll(field, -1, axis)
    return ahead - field


def diff_back(field, axis):
    if axis == 0:
        behind = jnp.concatenate([jnp.zeros_like(field[:1]), field[:-1]], axis=0)
    else:
        behind = jnp.roll(field, 1, axis)
    return field - behind


def curl_with(parts, differ):
    return (differ(parts[2], 1) - differ(parts[1], 2),
            differ(parts[0], 2) - differ(parts[2], 0),
            differ(parts[1], 0) - differ(parts[0], 1))


def evolve(current, omega, inv_eps, use_cos):
    zero = jnp.zeros(current.shape[1:], jnp.float32)
    electric = (zero, zero, zero)
    magnetic = (zero, zero, zero)
    stored = []
    for step in range(ITERS):
        phase = omega * (step + 1.0)
        signal = jnp.cos(phase) if use_cos else jnp.sin(phase)
        curl_e = curl_with(electric, diff_fwd)
        magnetic = tuple(magnetic[k] - COURANT * curl_e[k] for k in range(3))
        curl_h = curl_with(magnetic, diff_back)
        electric = tuple(electric[k] + COURANT * inv_eps * (curl_h[k] - current[k] * signal) for k in range(3))
        stored.append(electric)
    return stored


def reference(fwd_current, adj_current, inv_eps, wavelength, footprint):
    omegas = 0.25 + 0.05 * wavelength.astype(jnp.float32)

    def one_source(total, index):
        omega = omegas[index]
        forward = evolve(fwd_current[index], omega, inv_eps, False)
        adjoint = evolve(adj_current[index], omega, inv_eps, True)
        for step in range(ITERS):
            for k in range(3):
                total = total + forward[step][k] * adjoint[ITERS - 1 - step][k]
        return total, None

    start = jnp.zeros(inv_eps.shape, jnp.float32)
    grad, _ = lax.scan(one_source, start, jnp.arange(SOURCES, dtype=jnp.int32))
    flat = grad.reshape(NX * NY, NZ)
    return jax.ops.segment_sum(flat, footprint.reshape(NX * NY).astype(jnp.int32), num_segments=PIX)
```

```python
import jax
import jax.numpy as jnp
from jax import lax
from jax.experimental import pallas as pl
from jax.experimental.pallas import tpu as pltpu
from jax.sharding import PartitionSpec as P

ITERS = 4
PIX_DEV = 16
CAP = 4
F32 = jnp.float32


def y_next(a):
    return pltpu.roll(a, a.shape[0] - 1, 0)


def y_prev(a):
    return pltpu.roll(a, 1, 0)


def z_next(a):
    return pltpu.roll(a, a.shape[1] - 1, 1)


def z_prev(a):
    return pltpu.roll(a, 1, 1)


def curl_f(v, v2_next, v3_next):
    v1, v2, v3 = v
    h1 = (y_next(v3) - v3) - (z_next(v2) - v2)
    h2 = (z_next(v1) - v1) - (v3_next - v3)
    h3 = (v2_next - v2) - (y_next(v1) - v1)
    return h1, h2, h3


def scaled_curl_b(h, h2_prev, h3_prev, e):
    h1, h2, h3 = h
    return (
        e * ((h3 - y_prev(h3)) - (h2 - z_prev(h2))),
        e * ((h1 - z_prev(h1)) - (h3 - h3_prev)),
        e * ((h2 - h2_prev) - (h1 - y_prev(h1))),
    )


def edge_kernel(fwd, adj, eps, to_next, to_prev):
    last = eps.shape[0] - 1
    for run, current in enumerate((fwd, adj)):
        def source(i):
            e = -0.25 * eps[i]
            return tuple(e * current[0, c, i] for c in range(3))

        def put_next(k, v):
            to_next[run * 6 + k * 2] = v[2] + (z_next(v[0]) - v[0])
            to_next[run * 6 + k * 2 + 1] = v[1] + (y_next(v[0]) - v[0])

        def put_prev(k, v):
            to_prev[run * 6 + k * 2] = v[1]
            to_prev[run * 6 + k * 2 + 1] = v[2]

        a, b, c = source(last - 2), source(last - 1), source(last)
        put_next(0, c)
        zero = jnp.zeros_like(c[0])
        ha = curl_f(a, b[1], b[2])
        hb = curl_f(b, c[1], c[2])
        hc = curl_f(c, zero, zero)
        b = scaled_curl_b(hb, ha[1], ha[2], -0.25 * eps[last - 1])
        c = scaled_curl_b(hc, hb[1], hb[2], -0.25 * eps[last])
        put_next(1, c)
        hb = curl_f(b, c[1], c[2])
        hc = curl_f(c, zero, zero)
        put_next(2, scaled_curl_b(hc, hb[1], hb[2], -0.25 * eps[last]))

        a, b, c = source(0), source(1), source(2)
        put_prev(0, a)
        ha = curl_f(a, b[1], b[2])
        hb = curl_f(b, c[1], c[2])
        a1 = scaled_curl_b(ha, -a[2], a[1], -0.25 * eps[0])
        b1 = scaled_curl_b(hb, ha[1], ha[2], -0.25 * eps[1])
        put_prev(1, a1)
        ha = curl_f(a1, b1[1], b1[2])
        put_prev(2, scaled_curl_b(ha, -a1[2], a1[1], -0.25 * eps[0]))
    to_next[12] = -0.25 * eps[last]
    to_prev[12] = -0.25 * eps[0]


def pair_factors(sig):
    def by_step(s):
        s1, s2, s3, s4 = s
        return (
            (s1,),
            (s1 + s2, s1),
            (s1 + s2 + s3, 3.0 * s1 + s2, s1),
            (s1 + s2 + s3 + s4, 6.0 * s1 + 3.0 * s2 + s3, 5.0 * s1 + s2, s1),
        )

    f = by_step([sig[i] for i in range(ITERS)])
    a = by_step([sig[ITERS + i] for i in range(ITERS)])
    factors = {}
    for t in range(ITERS):
        for k, fk in enumerate(f[t]):
            for m, am in enumerate(a[ITERS - 1 - t]):
                factors[k, m] = factors.get((k, m), 0.0) + 4.0 * fk * am
    return factors


def field_kernel(sig, fwd, adj, eps, from_prev, from_next, out, v):
    planes = eps.shape[0]
    has_prev, has_next = sig[8], sig[9]
    e_prev, e_next = from_prev[12] * has_prev, from_next[12] * has_next
    factors = pair_factors(sig)

    def start(i, _):
        e = -0.25 * eps[i]
        for run, current in enumerate((fwd, adj)):
            for c in range(3):
                v[0, run, c, i] = e * current[0, c, i]
        return 0

    lax.fori_loop(0, planes, start, 0)
    zero = jnp.zeros(eps.shape[1:], F32)
    before = [(zero,) * 3, (zero,) * 3]
    after = [(zero,) * 3, (zero,) * 3]

    def read(k, run, i):
        return tuple(v[k, run, c, i] for c in range(3))

    for k in range(3):
        behind = []
        for run in range(2):
            c = before[run]
            h = curl_f(c, v[k, run, 1, 0], v[k, run, 2, 0])
            if k < 2:
                before[run] = scaled_curl_b(h, -c[2], c[1], e_prev)
            row = run * 6 + k * 2
            behind += [(h[1] + from_prev[row]) * has_prev, (h[2] - from_prev[row + 1]) * has_prev]

        def finish(i, new):
            if k < 2:
                for run in range(2):
                    for c in range(3):
                        v[k + 1, run, c, i] = new[run][c]
                return
            total = None
            for c in range(3):
                f = [v[j, 0, c, i] for j in range(3)] + [new[0][c]]
                a = [v[j, 1, c, i] for j in range(3)] + [new[1][c]]
                for m in range(4):
                    mix = None
                    for j in range(4 - m):
                        term = factors[j, m] * f[j]
                        mix = term if mix is None else mix + term
                    total = mix * a[m] if total is None else total + mix * a[m]
            for block in range(out.shape[0]):
                out[block, i] = total[block * 8 : block * 8 + 8]

        def plane(i, carry):
            e = -0.25 * eps[i]
            new, left = [], []
            for run in range(2):
                h = curl_f(read(k, run, i), v[k, run, 1, i + 1], v[k, run, 2, i + 1])
                new.append(scaled_curl_b(h, carry[2 * run], carry[2 * run + 1], e))
                left += [h[1], h[2]]
            finish(i, new)
            return tuple(left)

        carry = lax.fori_loop(0, planes - 1, plane, tuple(behind))
        last, new = planes - 1, []
        for run in range(2):
            d = after[run]
            own = curl_f(read(k, run, last), d[1], d[2])
            row = run * 6 + k * 2
            h = (own[0], own[1] - from_next[row + 1] * has_next, own[2] + from_next[row] * has_next)
            new.append(scaled_curl_b(h, carry[2 * run], carry[2 * run + 1], -0.25 * eps[last]))
            if k < 2:
                after[run] = scaled_curl_b(curl_f(d, zero, zero), own[1], own[2], e_next)
        finish(last, new)


def pack_kernel(owners, parts, fp_row, fp_col, out):
    count = parts.shape[1]
    summed = parts[0]
    for s in range(1, parts.shape[0]):
        summed = summed + parts[s]
    row_owner = (fp_row[...] >> 4) & (owners - 1)
    col_owner = (fp_col[...] >> 4) & (owners - 1)
    earlier = lax.broadcasted_iota(jnp.int32, (count, count), 0) < lax.broadcasted_iota(
        jnp.int32, (count, count), 1
    )
    same = (row_owner == col_owner) & earlier
    rank = jnp.sum(same.astype(jnp.int32), axis=0, keepdims=True)
    slot = row_owner * (2 * CAP) + rank
    rows = lax.broadcasted_iota(jnp.int32, (out.shape[0], count), 0)
    put = jnp.concatenate([(rows == slot).astype(F32), (rows == slot + CAP).astype(F32)], axis=1)
    pixel = (
        (fp_col[...] & (PIX_DEV - 1)) == lax.broadcasted_iota(jnp.int32, (count, summed.shape[1]), 1)
    ).astype(F32)
    out[...] = jnp.dot(
        put,
        jnp.concatenate([summed, pixel], axis=0),
        preferred_element_type=F32,
        precision=lax.Precision.HIGHEST,
    )


def pixel_kernel(arrived, out):
    got = arrived[...]
    rows = lax.broadcasted_iota(jnp.int32, got.shape, 0)
    is_data = (rows & (2 * CAP - 1)) < CAP
    pixel = jnp.where(is_data, pltpu.roll(got, got.shape[0] - CAP, 0), 0.0)
    sums = lax.dot_general(
        pixel,
        got,
        (((0,), (0,)), ((), ())),
        preferred_element_type=F32,
        precision=lax.Precision.HIGHEST,
    )
    out[...] = sums[: out.shape[0]]


def per_device(fwd_current, adj_current, inv_eps, wavelength, footprint):
    planes, ny, nz = inv_eps.shape
    space = lax.axis_size("space")
    groups = lax.axis_size("src")
    omega = 0.25 + 0.05 * wavelength.astype(F32)
    phases = omega * (jnp.arange(ITERS, dtype=F32) + 1.0)
    here = lax.axis_index("space")
    edges = jnp.stack([here > 0, here < space - 1]).astype(F32)
    sig = jnp.concatenate([jnp.sin(phases), jnp.cos(phases), edges])

    vmem = pl.BlockSpec(memory_space=pltpu.VMEM)
    smem = pl.BlockSpec(memory_space=pltpu.SMEM)
    trace = jax.ShapeDtypeStruct((13, ny, nz), F32)
    to_next, to_prev = pl.pallas_call(
        edge_kernel, out_shape=(trace, trace), in_specs=[vmem] * 3, out_specs=(vmem, vmem)
    )(fwd_current, adj_current, inv_eps)
    from_prev = lax.ppermute(to_next, "space", [(i, (i + 1) % space) for i in range(space)])
    from_next = lax.ppermute(to_prev, "space", [((i + 1) % space, i) for i in range(space)])
    width = ny // groups
    grad = pl.pallas_call(
        field_kernel,
        out_shape=jax.ShapeDtypeStruct((groups, planes, width, nz), F32),
        in_specs=[smem] + [vmem] * 5,
        out_specs=vmem,
        scratch_shapes=[pltpu.VMEM((3, 2, 3, planes, ny, nz), F32)],
        compiler_params=pltpu.CompilerParams(vmem_limit_bytes=48 * 1024 * 1024),
    )(sig, fwd_current, adj_current, inv_eps, from_prev, from_next)
    count = planes * width
    parts = lax.all_to_all(grad.reshape(groups, count, nz), "src", 0, 0, tiled=True)
    packed = pl.pallas_call(
        lambda *refs: pack_kernel(space, *refs),
        out_shape=jax.ShapeDtypeStruct((space * 2 * CAP, nz), F32),
        in_specs=[vmem] * 3,
        out_specs=vmem,
    )(parts, footprint.reshape(1, count), footprint.reshape(count, 1))
    arrived = lax.all_to_all(packed.reshape(space, 2 * CAP, nz), "space", 0, 0, tiled=True)
    return pl.pallas_call(
        pixel_kernel,
        out_shape=jax.ShapeDtypeStruct((PIX_DEV, nz), F32),
        in_specs=[vmem],
        out_specs=vmem,
    )(arrived.reshape(space * 2 * CAP, nz))


def solution(mesh):
    in_specs = (
        P("src", None, "space", None, None),
        P("src", None, "space", None, None),
        P("space", None, None),
        P("src"),
        P("space", "src"),
    )
    out_specs = P(("src", "space"), None)
    return jax.shard_map(
        per_device, mesh=mesh, in_specs=in_specs, out_specs=out_specs, check_vma=False
    )
```

```python
import jax
import jax.numpy as jnp
from jax import lax
from jax.experimental import pallas as pl
from jax.experimental.pallas import tpu as pltpu
from jax.sharding import PartitionSpec as P

ITERS = 4
PIX_DEV = 16
CAP = 4
DEPTH = 3
F32 = jnp.float32
BF16 = jnp.bfloat16
MIB = 1024 * 1024


def add(a, b):
    return b if a is None else a if b is None else a + b


def sub(a, b):
    return a if b is None else -b if a is None else a - b


def mul(a, b):
    return None if a is None or b is None else a * b


def y_ahead(a):
    return None if a is None else pltpu.roll(a, a.shape[0] - 1, 0) - a


def y_behind(a):
    return None if a is None else a - pltpu.roll(a, 1, 0)


def z_ahead(a):
    return None if a is None else pltpu.roll(a, a.shape[1] - 1, 1) - a


def z_behind(a):
    return None if a is None else a - pltpu.roll(a, 1, 1)


def curl_f(v, v2_next, v3_next):
    v1, v2, v3 = v
    z1, z2 = z_ahead(v1), z_ahead(v2)
    h2 = sub(z1, sub(v3_next, v3))
    h1 = sub(y_ahead(v3), z2)
    h3 = sub(sub(v2_next, v2), y_ahead(v1))
    return h1, h2, h3


def scaled_curl_b(h, h2_prev, h3_prev, e):
    h1, h2, h3 = h
    z1, z2 = z_behind(h1), z_behind(h2)
    return (
        mul(e, sub(y_behind(h3), z2)),
        mul(e, sub(z1, sub(h3, h3_prev))),
        mul(e, sub(sub(h2, h2_prev), y_behind(h1))),
    )


E_ROW = 4
SPANS = ((0, 5), (5, 4), (9, 4))


def trace_row(run, k):
    return SPANS[k][0] + 2 * run


def edge_kernel(
    fwd_hbm, adj_hbm, eps_hbm, next_hbm, prev_hbm, current, eps, to_next, to_prev, sem, out_sem
):
    last = eps_hbm.shape[0] - 1
    runs = range(2)
    copies = []
    for at in (0, last + 1 - DEPTH):
        span = pl.ds(at, DEPTH)
        copies.append((eps_hbm.at[span], eps.at[span]))
        for run, whole in enumerate((fwd_hbm, adj_hbm)):
            copies.append((whole.at[0, :, span], current.at[run, :, span]))
    copies = [pltpu.make_async_copy(a, b, sem.at[n]) for n, (a, b) in enumerate(copies)]
    for copy in copies:
        copy.start()
    for copy in copies:
        copy.wait()

    def source(run, i):
        e = -0.25 * eps[i]
        return tuple(e * current[run, c, i] for c in range(3))

    def put_next(run, k, v):
        to_next[trace_row(run, k)] = v[2] + z_ahead(v[0])
        to_next[trace_row(run, k) + 1] = v[1] + y_ahead(v[0])

    def put_prev(run, k, v):
        to_prev[trace_row(run, k)] = v[1]
        to_prev[trace_row(run, k) + 1] = v[2]

    sent = []

    def send(k):
        span = pl.ds(*SPANS[k])
        for n, (a, b) in enumerate(((to_next, next_hbm), (to_prev, prev_hbm))):
            sent.append(pltpu.make_async_copy(a.at[span], b.at[span], out_sem.at[2 * k + n]))
            sent[-1].start()

    end = [[source(r, last - 2), source(r, last - 1), source(r, last)] for r in runs]
    first = [[source(r, 0), source(r, 1), source(r, 2)] for r in runs]
    for r in runs:
        put_next(r, 0, end[r][2])
        put_prev(r, 0, first[r][0])
    to_next[E_ROW] = -0.25 * eps[last]
    to_prev[E_ROW] = -0.25 * eps[0]
    send(0)
    end_h = [
        [curl_f(a, b[1], b[2]), curl_f(b, c[1], c[2]), curl_f(c, None, None)] for a, b, c in end
    ]
    first_h = [[curl_f(a, b[1], b[2]), curl_f(b, c[1], c[2])] for a, b, c in first]
    end1 = [
        [
            scaled_curl_b(hb, ha[1], ha[2], -0.25 * eps[last - 1]),
            scaled_curl_b(hc, hb[1], hb[2], -0.25 * eps[last]),
        ]
        for ha, hb, hc in end_h
    ]
    first1 = [
        [
            scaled_curl_b(ha, -v[0][2], v[0][1], -0.25 * eps[0]),
            scaled_curl_b(hb, ha[1], ha[2], -0.25 * eps[1]),
        ]
        for (ha, hb), v in zip(first_h, first)
    ]
    for r in runs:
        put_next(r, 1, end1[r][1])
        put_prev(r, 1, first1[r][0])
    send(1)
    end_h = [[curl_f(b, c[1], c[2]), curl_f(c, None, None)] for b, c in end1]
    first_h = [curl_f(a, b[1], b[2]) for a, b in first1]
    end2 = [scaled_curl_b(hc, hb[1], hb[2], -0.25 * eps[last]) for hb, hc in end_h]
    first2 = [
        scaled_curl_b(h, -v[0][2], v[0][1], -0.25 * eps[0]) for h, v in zip(first_h, first1)
    ]
    for r in runs:
        put_next(r, 2, end2[r])
        put_prev(r, 2, first2[r])
    send(2)
    for copy in sent:
        copy.wait()


def pair_factors(sig):
    def by_step(s):
        s1, s2, s3, s4 = s
        return (
            (s1,),
            (s1 + s2, s1),
            (s1 + s2 + s3, 3.0 * s1 + s2, s1),
            (s1 + s2 + s3 + s4, 6.0 * s1 + 3.0 * s2 + s3, 5.0 * s1 + s2, s1),
        )

    f = by_step([sig[i] for i in range(ITERS)])
    a = by_step([sig[ITERS + i] for i in range(ITERS)])
    factors = {}
    for t in range(ITERS):
        for k, fk in enumerate(f[t]):
            for m, am in enumerate(a[ITERS - 1 - t]):
                factors[k, m] = factors.get((k, m), 0.0) + 4.0 * fk * am
    return factors


REACHED = tuple((depth, k) for depth in range(DEPTH) for k in range(depth + 1, DEPTH + 1))


def own_kernel(sig, fwd, adj, eps, fp_row, fp_col, out, near, mixes, put, v):
    planes = eps.shape[0]
    last = planes - 1
    has_prev = sig[8]
    factors = pair_factors(sig)

    def start(i, _):
        e = -0.25 * eps[i]
        for run, current in enumerate((fwd, adj)):
            for c in range(3):
                v[0, run, c, i] = e * current[0, c, i]
        return 0

    lax.fori_loop(0, planes, start, 0)

    def read(k, run, i):
        return tuple(v[k, run, c, i] for c in range(3))

    for k in range(DEPTH):
        behind = []
        for run in range(2):
            if k < 2:
                near[run, 2 * k] = v[k, run, 1, 0]
                near[run, 2 * k + 1] = v[k, run, 2, 0]
            behind += [v[k, run, 2, 0] * -has_prev, v[k, run, 1, 0] * has_prev]

        def finish(i, new):
            if k < 2:
                for run in range(2):
                    for c in range(3):
                        v[k + 1, run, c, i] = new[run][c]
                return
            total = None
            for c in range(3):
                f = [v[j, 0, c, i] for j in range(DEPTH)] + [new[0][c]]
                a = [v[j, 1, c, i] for j in range(DEPTH)] + [new[1][c]]
                for m in range(4):
                    mix = None
                    for j in range(4 - m):
                        mix = add(mix, factors[j, m] * f[j])
                    total = add(total, mix * a[m])
            for block in range(out.shape[0]):
                out[block, i] = total[block * 8 : block * 8 + 8]

        def plane(i, carry):
            e = -0.25 * eps[i]
            h = [curl_f(read(k, r, i), v[k, r, 1, i + 1], v[k, r, 2, i + 1]) for r in range(2)]
            finish(i, [scaled_curl_b(h[r], carry[2 * r], carry[2 * r + 1], e) for r in range(2)])
            return h[0][1], h[0][2], h[1][1], h[1][2]

        carry = lax.fori_loop(0, last, plane, tuple(behind))
        new = []
        for run in range(2):
            h = curl_f(read(k, run, last), None, None)
            if k < 2:
                near[run, 4 + 2 * k] = h[1]
                near[run, 5 + 2 * k] = h[2]
            new.append(scaled_curl_b(h, carry[2 * run], carry[2 * run + 1], -0.25 * eps[last]))
        finish(last, new)

    for side in range(2):
        for n, (depth, k) in enumerate(REACHED):
            i = last - depth if side else depth
            for c in range(3):
                for run in range(2):
                    mix = None
                    for j in range(4 - k):
                        factor = factors[(j, k) if run else (k, j)]
                        mix = add(mix, factor * v[j, 1 - run, c, i])
                    mixes[side, run, n, c] = mix

    count = fp_row.shape[1]
    owners = put.shape[0] // (2 * CAP)
    row_owner = (fp_row[...] >> 4) & (owners - 1)
    col_owner = (fp_col[...] >> 4) & (owners - 1)
    earlier = lax.broadcasted_iota(jnp.int32, (count, count), 0) < lax.broadcasted_iota(
        jnp.int32, (count, count), 1
    )
    same = (row_owner == col_owner) & earlier
    rank = jnp.sum(same.astype(F32), axis=0, keepdims=True).astype(jnp.int32)
    slot = row_owner * (2 * CAP) + rank
    rows = lax.broadcasted_iota(jnp.int32, (put.shape[0], count), 0)
    value = (rows == slot).astype(F32)
    mark = (rows == slot + CAP).astype(F32)
    put[...] = jnp.concatenate([value, value, value, mark], axis=1).astype(BF16)


def join_kernel(sig, eps, grad, near, mixes, from_prev, from_next, out):
    last = eps.shape[0] - 1
    has_prev, has_next = sig[8], sig[9]
    runs = range(2)
    e_prev, e_next = from_prev[E_ROW] * has_prev, from_next[E_ROW] * has_next
    e = {i: -0.25 * eps[i] for i in (0, 1, 2, last - 2, last - 1, last)}
    factors = pair_factors(sig)

    def left_trace(r, k):
        row = trace_row(r, k)
        return from_prev[row] * has_prev, from_prev[row + 1] * -has_prev

    def right_trace(r, k):
        row = trace_row(r, k)
        return from_next[row + 1] * -has_next, from_next[row] * has_next

    def passed(h, e):
        return None, e * h[1], -e * h[0]

    t = [left_trace(r, 0) for r in runs]
    u = [right_trace(r, 0) for r in runs]
    own = [(None, -near[r, 1], near[r, 0]) for r in runs]
    c = [scaled_curl_b(own[r], None, None, e_prev) for r in runs]
    g1 = [scaled_curl_b((None, *u[r]), None, None, e[last]) for r in runs]
    f1 = [passed(t[r], e[0]) for r in runs]
    d = [passed((near[r, 4], near[r, 5]), e_next) for r in runs]
    h0 = [curl_f(f1[r], None, None) for r in runs]
    hm = [curl_f(c[r], f1[r][1], f1[r][2]) for r in runs]
    hd = [curl_f(d[r], None, None) for r in runs]
    h7 = [curl_f(g1[r], d[r][1], d[r][2]) for r in runs]
    h6 = [(-g1[r][2], g1[r][1]) for r in runs]
    t = [left_trace(r, 1) for r in runs]
    u = [right_trace(r, 1) for r in runs]
    f2a = [scaled_curl_b(h0[r], hm[r][1] + t[r][0], hm[r][2] + t[r][1], e[0]) for r in runs]
    c = [
        scaled_curl_b(
            (hm[r][0], hm[r][1] - near[r, 3], hm[r][2] + near[r, 2]), -c[r][2], c[r][1], e_prev
        )
        for r in runs
    ]
    f2b = [passed(h0[r][1:], e[1]) for r in runs]
    g2a = [
        scaled_curl_b((h7[r][0], h7[r][1] + u[r][0], h7[r][2] + u[r][1]), *h6[r], e[last])
        for r in runs
    ]
    g2b = [scaled_curl_b((None, *h6[r]), None, None, e[last - 1]) for r in runs]
    d = [
        scaled_curl_b(hd[r], near[r, 6] + h7[r][1], near[r, 7] + h7[r][2], e_next) for r in runs
    ]
    h0 = [curl_f(f2a[r], f2b[r][1], f2b[r][2]) for r in runs]
    h1 = [curl_f(f2b[r], None, None) for r in runs]
    hm = [curl_f(c[r], f2a[r][1], f2a[r][2]) for r in runs]
    h7 = [curl_f(g2a[r], d[r][1], d[r][2]) for r in runs]
    h6 = [curl_f(g2b[r], g2a[r][1], g2a[r][2]) for r in runs]
    h5 = [(-g2b[r][2], g2b[r][1]) for r in runs]
    t = [left_trace(r, 2) for r in runs]
    u = [right_trace(r, 2) for r in runs]
    f3a = [scaled_curl_b(h0[r], hm[r][1] + t[r][0], hm[r][2] + t[r][1], e[0]) for r in runs]
    f3b = [scaled_curl_b(h1[r], h0[r][1], h0[r][2], e[1]) for r in runs]
    f3c = [passed(h1[r][1:], e[2]) for r in runs]
    g3a = [
        scaled_curl_b(
            (h7[r][0], h7[r][1] + u[r][0], h7[r][2] + u[r][1]), h6[r][1], h6[r][2], e[last]
        )
        for r in runs
    ]
    g3b = [scaled_curl_b(h6[r], *h5[r], e[last - 1]) for r in runs]
    g3c = [scaled_curl_b((None, *h5[r]), None, None, e[last - 2]) for r in runs]

    fields = (
        ({(0, 1): f1, (0, 2): f2a, (0, 3): f3a, (1, 2): f2b, (1, 3): f3b, (2, 3): f3c}),
        ({(0, 1): g1, (0, 2): g2a, (0, 3): g3a, (1, 2): g2b, (1, 3): g3b, (2, 3): g3c}),
    )
    for i in range(DEPTH, last + 1 - DEPTH):
        for block in range(out.shape[0]):
            out[block, i] = grad[block, i]
    for side in range(2):
        for depth in range(DEPTH):
            i = last - depth if side else depth
            total = None
            for n, (at, k) in enumerate(REACHED):
                if at == depth:
                    f = fields[side][at, k]
                    for x in range(3):
                        for r in runs:
                            if f[r][x] is not None:
                                total = add(total, f[r][x] * mixes[side, r, n, x])
            if depth == 0:
                one, two = fields[side][0, 1], fields[side][0, 2]
                for x in range(3):
                    if one[0][x] is not None:
                        both = factors[1, 1] * one[1][x] + factors[1, 2] * two[1][x]
                        total = total + one[0][x] * both
                        total = total + two[0][x] * (factors[2, 1] * one[1][x])
            for block in range(out.shape[0]):
                out[block, i] = grad[block, i] + total[block * 8 : block * 8 + 8]


def in_thirds(a):
    high = a.astype(BF16)
    rest = a - high.astype(F32)
    middle = rest.astype(BF16)
    return high, middle, (rest - middle.astype(F32)).astype(BF16)


def pack_kernel(parts, put, fp_col, out):
    count = parts.shape[1]
    summed = parts[0]
    for s in range(1, parts.shape[0]):
        summed = summed + parts[s]
    lanes = lax.broadcasted_iota(jnp.int32, (count, summed.shape[1]), 1)
    pixel = ((fp_col[...] & (PIX_DEV - 1)) == lanes).astype(F32).astype(BF16)
    rows = jnp.concatenate([*in_thirds(summed), pixel], axis=0)
    out[...] = jnp.dot(put[...], rows, preferred_element_type=F32)


def pixel_kernel(arrived, out):
    got = arrived[...]
    rows = lax.broadcasted_iota(jnp.int32, got.shape, 0)
    is_data = (rows & (2 * CAP - 1)) < CAP
    pixel = jnp.where(is_data, pltpu.roll(got, got.shape[0] - CAP, 0), 0.0).astype(BF16)
    sums = None
    for part in in_thirds(got):
        sums = add(
            sums,
            lax.dot_general(pixel, part, (((0,), (0,)), ((), ())), preferred_element_type=F32),
        )
    out[...] = sums[: out.shape[0]]


def per_device(fwd_current, adj_current, inv_eps, wavelength, footprint):
    planes, ny, nz = inv_eps.shape
    space = lax.axis_size("space")
    groups = lax.axis_size("src")
    width = ny // groups
    count = planes * width
    omega = 0.25 + 0.05 * wavelength.astype(F32)
    phases = omega * (jnp.arange(ITERS, dtype=F32) + 1.0)
    here = lax.axis_index("space")
    edges = jnp.stack([here > 0, here < space - 1]).astype(F32)
    sig = jnp.concatenate([jnp.sin(phases), jnp.cos(phases), edges])
    fp_row, fp_col = footprint.reshape(1, count), footprint.reshape(count, 1)

    vmem = pl.BlockSpec(memory_space=pltpu.VMEM)
    smem = pl.BlockSpec(memory_space=pltpu.SMEM)
    hbm = pl.BlockSpec(memory_space=pltpu.HBM)

    def array(*shape, dtype=F32):
        return jax.ShapeDtypeStruct(shape, dtype)

    def call(kernel, outs, mib, args, scratch=(), held=vmem):
        return pl.pallas_call(
            kernel,
            out_shape=outs,
            in_specs=[smem if a is sig else held for a in args],
            out_specs=(held,) * len(outs),
            scratch_shapes=scratch,
            compiler_params=pltpu.CompilerParams(vmem_limit_bytes=mib * MIB),
        )(*args)

    to_next, to_prev = call(
        edge_kernel,
        (array(13, ny, nz), array(13, ny, nz)),
        60,
        (fwd_current, adj_current, inv_eps),
        [
            pltpu.VMEM((2, 3, planes, ny, nz), F32),
            pltpu.VMEM((planes, ny, nz), F32),
            pltpu.VMEM((13, ny, nz), F32),
            pltpu.VMEM((13, ny, nz), F32),
            pltpu.SemaphoreType.DMA((6,)),
            pltpu.SemaphoreType.DMA((6,)),
        ],
        hbm,
    )
    from_prev = lax.ppermute(to_next, "space", [(i, (i + 1) % space) for i in range(space)])
    from_next = lax.ppermute(to_prev, "space", [((i + 1) % space, i) for i in range(space)])
    grad, near, mixes, put = call(
        own_kernel,
        (
            array(groups, planes, width, nz),
            array(2, 8, ny, nz),
            array(2, 2, len(REACHED), 3, ny, nz),
            array(space * 2 * CAP, 4 * count, dtype=BF16),
        ),
        20,
        (sig, fwd_current, adj_current, inv_eps, fp_row, fp_col),
        [
            pltpu.VMEM((3, 2, 3, planes, ny, nz), F32),
        ],
    )
    (grad,) = call(
        join_kernel,
        (array(groups, planes, width, nz),),
        16,
        (sig, inv_eps, grad, near, mixes, from_prev, from_next),
    )
    parts = lax.all_to_all(grad.reshape(groups, count, nz), "src", 0, 0, tiled=True)
    (packed,) = call(pack_kernel, (array(space * 2 * CAP, nz),), 4, (parts, put, fp_col))
    arrived = lax.all_to_all(packed.reshape(space, 2 * CAP, nz), "space", 0, 0, tiled=True)
    (sums,) = call(
        pixel_kernel, (array(PIX_DEV, nz),), 4, (arrived.reshape(space * 2 * CAP, nz),)
    )
    return sums


def solution(mesh):
    in_specs = (
        P("src", None, "space", None, None),
        P("src", None, "space", None, None),
        P("space", None, None),
        P("src"),
        P("space", "src"),
    )
    out_specs = P(("src", "space"), None)
    return jax.shard_map(
        per_device, mesh=mesh, in_specs=in_specs, out_specs=out_specs, check_vma=False
    )
```

```python
import functools

import jax
import jax.numpy as jnp
from jax import lax
from jax.experimental import pallas as pl
from jax.experimental.pallas import tpu as pltpu
from jax.sharding import PartitionSpec as P

ITERS = 4
PIX_DEV = 16
CAP = 4
DEPTH = 3
F32 = jnp.float32
BF16 = jnp.bfloat16
MIB = 1024 * 1024


def add(a, b):
    return b if a is None else a if b is None else a + b


def sub(a, b):
    return a if b is None else -b if a is None else a - b


def mul(a, b):
    return None if a is None or b is None else a * b


def y_ahead(a):
    return None if a is None else pltpu.roll(a, a.shape[0] - 1, 0) - a


def y_behind(a):
    return None if a is None else a - pltpu.roll(a, 1, 0)


def z_ahead(a):
    return None if a is None else pltpu.roll(a, a.shape[1] - 1, 1) - a


def z_behind(a):
    return None if a is None else a - pltpu.roll(a, 1, 1)


def curl_f(v, v2_next, v3_next):
    v1, v2, v3 = v
    z1, z2 = z_ahead(v1), z_ahead(v2)
    h2 = sub(z1, sub(v3_next, v3))
    h1 = sub(y_ahead(v3), z2)
    h3 = sub(sub(v2_next, v2), y_ahead(v1))
    return h1, h2, h3


def scaled_curl_b(h, h2_prev, h3_prev, e):
    h1, h2, h3 = h
    z1, z2 = z_behind(h1), z_behind(h2)
    return (
        mul(e, sub(y_behind(h3), z2)),
        mul(e, sub(z1, sub(h3, h3_prev))),
        mul(e, sub(sub(h2, h2_prev), y_behind(h1))),
    )


E_ROW = 12


def trace_row(run, k):
    return 6 * run + 2 * k


def next_is_partner(on_chip):
    return (lax.axis_index("space") % 2 == 0) == on_chip


def edge_kernel(on_chip, fwd_hbm, adj_hbm, eps_hbm, traces, current, eps, sem):
    to_next = next_is_partner(on_chip)
    span = pl.ds(jnp.where(to_next, eps_hbm.shape[0] - DEPTH, 0), DEPTH)
    copies = [(eps_hbm.at[span], eps)]
    for run, whole in enumerate((fwd_hbm, adj_hbm)):
        copies.append((whole.at[0, :, span], current.at[run]))
    copies = [pltpu.make_async_copy(a, b, sem.at[n]) for n, (a, b) in enumerate(copies)]
    for copy in copies:
        copy.start()
    for copy in copies:
        copy.wait()

    def sources():
        e = [-0.25 * eps[i] for i in range(DEPTH)]
        v = [
            [tuple(e[i] * current[run, c, i] for c in range(3)) for i in range(DEPTH)]
            for run in range(2)
        ]
        return e, v

    @pl.when(to_next)
    def _():
        def put(k, plane):
            for run, v in enumerate(plane):
                traces[trace_row(run, k)] = v[2] + z_ahead(v[0])
                traces[trace_row(run, k) + 1] = v[1] + y_ahead(v[0])

        e, v = sources()
        traces[E_ROW] = e[2]
        put(0, [c for _, _, c in v])
        h = [(curl_f(a, b[1], b[2]), curl_f(b, c[1], c[2]), curl_f(c, None, None)) for a, b, c in v]
        v = [
            (scaled_curl_b(hb, ha[1], ha[2], e[1]), scaled_curl_b(hc, hb[1], hb[2], e[2]))
            for ha, hb, hc in h
        ]
        put(1, [c for _, c in v])
        h = [(curl_f(b, c[1], c[2]), curl_f(c, None, None)) for b, c in v]
        put(2, [scaled_curl_b(hc, hb[1], hb[2], e[2]) for hb, hc in h])

    @pl.when(jnp.logical_not(to_next))
    def _():
        def put(k, plane):
            for run, v in enumerate(plane):
                traces[trace_row(run, k)] = v[1]
                traces[trace_row(run, k) + 1] = v[2]

        e, v = sources()
        traces[E_ROW] = e[0]
        put(0, [a for a, _, _ in v])
        h = [(curl_f(a, b[1], b[2]), curl_f(b, c[1], c[2])) for a, b, c in v]
        v = [
            (scaled_curl_b(ha, -a[2], a[1], e[0]), scaled_curl_b(hb, ha[1], ha[2], e[1]))
            for (ha, hb), (a, _, _) in zip(h, v)
        ]
        put(1, [a for a, _ in v])
        h = [curl_f(a, b[1], b[2]) for a, b in v]
        put(2, [scaled_curl_b(ha, -a[2], a[1], e[0]) for ha, (a, _) in zip(h, v)])


def pair_factors(sig):
    def by_step(s):
        s1, s2, s3, s4 = s
        return (
            (s1,),
            (s1 + s2, s1),
            (s1 + s2 + s3, 3.0 * s1 + s2, s1),
            (s1 + s2 + s3 + s4, 6.0 * s1 + 3.0 * s2 + s3, 5.0 * s1 + s2, s1),
        )

    f = by_step([sig[i] for i in range(ITERS)])
    a = by_step([sig[ITERS + i] for i in range(ITERS)])
    factors = {}
    for t in range(ITERS):
        for k, fk in enumerate(f[t]):
            for m, am in enumerate(a[ITERS - 1 - t]):
                factors[k, m] = factors.get((k, m), 0.0) + 4.0 * fk * am
    return factors


REACHED = tuple((depth, k) for depth in range(DEPTH) for k in range(depth + 1, DEPTH + 1))


def own_kernel(
    sig, fwd_hbm, adj_hbm, eps_hbm, footprint, out, near, mixes, put, pixel, v, fwd, adj, eps, sem
):
    pairs = ((fwd_hbm, fwd), (adj_hbm, adj), (eps_hbm, eps))
    copies = [pltpu.make_async_copy(a, b, sem.at[n]) for n, (a, b) in enumerate(pairs)]
    for copy in copies:
        copy.start()
    for copy in copies:
        copy.wait()
    planes = eps.shape[0]
    last = planes - 1
    has_prev = sig[8]
    factors = pair_factors(sig)

    def start(i, _):
        e = -0.25 * eps[i]
        for run, current in enumerate((fwd, adj)):
            for c in range(3):
                v[0, run, c, i] = e * current[0, c, i]
        return 0

    lax.fori_loop(0, planes, start, 0)

    def read(k, run, i):
        return tuple(v[k, run, c, i] for c in range(3))

    for k in range(DEPTH):
        behind = []
        for run in range(2):
            if k < 2:
                near[run, 2 * k] = v[k, run, 1, 0]
                near[run, 2 * k + 1] = v[k, run, 2, 0]
            behind += [v[k, run, 2, 0] * -has_prev, v[k, run, 1, 0] * has_prev]

        def finish(i, new):
            if k < 2:
                for run in range(2):
                    for c in range(3):
                        v[k + 1, run, c, i] = new[run][c]
                return
            total = None
            for c in range(3):
                f = [v[j, 0, c, i] for j in range(DEPTH)] + [new[0][c]]
                a = [v[j, 1, c, i] for j in range(DEPTH)] + [new[1][c]]
                for m in range(4):
                    mix = None
                    for j in range(4 - m):
                        mix = add(mix, factors[j, m] * f[j])
                    total = add(total, mix * a[m])
            for block in range(out.shape[0]):
                out[block, i] = total[block * 8 : block * 8 + 8]

        def plane(i, carry):
            e = -0.25 * eps[i]
            h = [curl_f(read(k, r, i), v[k, r, 1, i + 1], v[k, r, 2, i + 1]) for r in range(2)]
            finish(i, [scaled_curl_b(h[r], carry[2 * r], carry[2 * r + 1], e) for r in range(2)])
            return h[0][1], h[0][2], h[1][1], h[1][2]

        carry = lax.fori_loop(0, last, plane, tuple(behind))
        new = []
        for run in range(2):
            h = curl_f(read(k, run, last), None, None)
            if k < 2:
                near[run, 4 + 2 * k] = h[1]
                near[run, 5 + 2 * k] = h[2]
            new.append(scaled_curl_b(h, carry[2 * run], carry[2 * run + 1], -0.25 * eps[last]))
        finish(last, new)

    for side in range(2):
        for n, (depth, k) in enumerate(REACHED):
            i = last - depth if side else depth
            for c in range(3):
                for run in range(2):
                    mix = None
                    for j in range(4 - k):
                        factor = factors[(j, k) if run else (k, j)]
                        mix = add(mix, factor * v[j, 1 - run, c, i])
                    mixes[side, run, n, c] = mix

    wide, width = footprint.shape
    count = wide * width
    owners = put.shape[0] // (2 * CAP)
    ids = footprint[...]
    by_row = jnp.concatenate(
        [jnp.broadcast_to(ids[i : i + 1], (width, width)) for i in range(wide)], axis=0
    ).astype(F32)
    at = lax.broadcasted_iota(jnp.int32, (count, width), 0) % width
    own = at == lax.broadcasted_iota(jnp.int32, (count, width), 1)
    col = jnp.sum(jnp.where(own, by_row, 0.0), axis=1, keepdims=True)
    diagonal = lax.broadcasted_iota(jnp.int32, (count, count), 0) == lax.broadcasted_iota(
        jnp.int32, (count, count), 1
    )
    row = jnp.sum(jnp.where(diagonal, col, 0.0), axis=0, keepdims=True)
    row, col = row.astype(jnp.int32), col.astype(jnp.int32)
    lanes = lax.broadcasted_iota(jnp.int32, pixel.shape, 1)
    pixel[...] = ((col & (PIX_DEV - 1)) == lanes).astype(F32).astype(BF16)
    row_owner = (row >> 4) & (owners - 1)
    col_owner = (col >> 4) & (owners - 1)
    earlier = lax.broadcasted_iota(jnp.int32, (count, count), 0) < lax.broadcasted_iota(
        jnp.int32, (count, count), 1
    )
    same = (row_owner == col_owner) & earlier
    rank = jnp.sum(same.astype(F32), axis=0, keepdims=True).astype(jnp.int32)
    slot = row_owner * (2 * CAP) + rank
    rows = lax.broadcasted_iota(jnp.int32, (put.shape[0], count), 0)
    value = (rows == slot).astype(F32)
    mark = (rows == slot + CAP).astype(F32)
    put[...] = jnp.concatenate([value, value, value, mark], axis=1).astype(BF16)


def join_kernel(sig, eps, grad, near, mixes, from_ring, from_chip, out):
    last = eps.shape[0] - 1
    has_prev, has_next = sig[8], sig[9]
    runs = range(2)
    first_of_pair = lax.axis_index("space") % 2 == 0

    def from_prev(row):
        return jnp.where(first_of_pair, from_ring[row], from_chip[row])

    def from_next(row):
        return jnp.where(first_of_pair, from_chip[row], from_ring[row])

    e_prev, e_next = from_prev(E_ROW) * has_prev, from_next(E_ROW) * has_next
    e = {i: -0.25 * eps[i] for i in (0, 1, 2, last - 2, last - 1, last)}
    factors = pair_factors(sig)

    def left_trace(r, k):
        row = trace_row(r, k)
        return from_prev(row) * has_prev, from_prev(row + 1) * -has_prev

    def right_trace(r, k):
        row = trace_row(r, k)
        return from_next(row + 1) * -has_next, from_next(row) * has_next

    def passed(h, e):
        return None, e * h[1], -e * h[0]

    t = [left_trace(r, 0) for r in runs]
    u = [right_trace(r, 0) for r in runs]
    own = [(None, -near[r, 1], near[r, 0]) for r in runs]
    c = [scaled_curl_b(own[r], None, None, e_prev) for r in runs]
    g1 = [scaled_curl_b((None, *u[r]), None, None, e[last]) for r in runs]
    f1 = [passed(t[r], e[0]) for r in runs]
    d = [passed((near[r, 4], near[r, 5]), e_next) for r in runs]
    h0 = [curl_f(f1[r], None, None) for r in runs]
    hm = [curl_f(c[r], f1[r][1], f1[r][2]) for r in runs]
    hd = [curl_f(d[r], None, None) for r in runs]
    h7 = [curl_f(g1[r], d[r][1], d[r][2]) for r in runs]
    h6 = [(-g1[r][2], g1[r][1]) for r in runs]
    t = [left_trace(r, 1) for r in runs]
    u = [right_trace(r, 1) for r in runs]
    f2a = [scaled_curl_b(h0[r], hm[r][1] + t[r][0], hm[r][2] + t[r][1], e[0]) for r in runs]
    c = [
        scaled_curl_b(
            (hm[r][0], hm[r][1] - near[r, 3], hm[r][2] + near[r, 2]), -c[r][2], c[r][1], e_prev
        )
        for r in runs
    ]
    f2b = [passed(h0[r][1:], e[1]) for r in runs]
    g2a = [
        scaled_curl_b((h7[r][0], h7[r][1] + u[r][0], h7[r][2] + u[r][1]), *h6[r], e[last])
        for r in runs
    ]
    g2b = [scaled_curl_b((None, *h6[r]), None, None, e[last - 1]) for r in runs]
    d = [
        scaled_curl_b(hd[r], near[r, 6] + h7[r][1], near[r, 7] + h7[r][2], e_next) for r in runs
    ]
    h0 = [curl_f(f2a[r], f2b[r][1], f2b[r][2]) for r in runs]
    h1 = [curl_f(f2b[r], None, None) for r in runs]
    hm = [curl_f(c[r], f2a[r][1], f2a[r][2]) for r in runs]
    h7 = [curl_f(g2a[r], d[r][1], d[r][2]) for r in runs]
    h6 = [curl_f(g2b[r], g2a[r][1], g2a[r][2]) for r in runs]
    h5 = [(-g2b[r][2], g2b[r][1]) for r in runs]
    t = [left_trace(r, 2) for r in runs]
    u = [right_trace(r, 2) for r in runs]
    f3a = [scaled_curl_b(h0[r], hm[r][1] + t[r][0], hm[r][2] + t[r][1], e[0]) for r in runs]
    f3b = [scaled_curl_b(h1[r], h0[r][1], h0[r][2], e[1]) for r in runs]
    f3c = [passed(h1[r][1:], e[2]) for r in runs]
    g3a = [
        scaled_curl_b(
            (h7[r][0], h7[r][1] + u[r][0], h7[r][2] + u[r][1]), h6[r][1], h6[r][2], e[last]
        )
        for r in runs
    ]
    g3b = [scaled_curl_b(h6[r], *h5[r], e[last - 1]) for r in runs]
    g3c = [scaled_curl_b((None, *h5[r]), None, None, e[last - 2]) for r in runs]

    fields = (
        ({(0, 1): f1, (0, 2): f2a, (0, 3): f3a, (1, 2): f2b, (1, 3): f3b, (2, 3): f3c}),
        ({(0, 1): g1, (0, 2): g2a, (0, 3): g3a, (1, 2): g2b, (1, 3): g3b, (2, 3): g3c}),
    )
    for i in range(DEPTH, last + 1 - DEPTH):
        for block in range(out.shape[0]):
            out[block, i] = grad[block, i]
    for side in range(2):
        for depth in range(DEPTH):
            i = last - depth if side else depth
            total = None
            for n, (at, k) in enumerate(REACHED):
                if at == depth:
                    f = fields[side][at, k]
                    for x in range(3):
                        for r in runs:
                            if f[r][x] is not None:
                                total = add(total, f[r][x] * mixes[side, r, n, x])
            if depth == 0:
                one, two = fields[side][0, 1], fields[side][0, 2]
                for x in range(3):
                    if one[0][x] is not None:
                        both = factors[1, 1] * one[1][x] + factors[1, 2] * two[1][x]
                        total = total + one[0][x] * both
                        total = total + two[0][x] * (factors[2, 1] * one[1][x])
            for block in range(out.shape[0]):
                out[block, i] = grad[block, i] + total[block * 8 : block * 8 + 8]


def in_thirds(a):
    high = a.astype(BF16)
    rest = a - high.astype(F32)
    middle = rest.astype(BF16)
    return high, middle, (rest - middle.astype(F32)).astype(BF16)


def pack_kernel(parts, put, pixel, out):
    summed = parts[0]
    for s in range(1, parts.shape[0]):
        summed = summed + parts[s]
    rows = jnp.concatenate([*in_thirds(summed), pixel[...]], axis=0)
    out[...] = jnp.dot(put[...], rows, preferred_element_type=F32)


def pixel_kernel(arrived, out):
    got = arrived[...]
    rows = lax.broadcasted_iota(jnp.int32, got.shape, 0)
    is_data = (rows & (2 * CAP - 1)) < CAP
    pixel = jnp.where(is_data, pltpu.roll(got, got.shape[0] - CAP, 0), 0.0).astype(BF16)
    sums = None
    for part in in_thirds(got):
        sums = add(
            sums,
            lax.dot_general(pixel, part, (((0,), (0,)), ((), ())), preferred_element_type=F32),
        )
    out[...] = sums[: out.shape[0]]


def per_device(fwd_current, adj_current, inv_eps, wavelength, footprint):
    planes, ny, nz = inv_eps.shape
    space = lax.axis_size("space")
    groups = lax.axis_size("src")
    width = ny // groups
    count = planes * width
    omega = 0.25 + 0.05 * wavelength.astype(F32)
    phases = omega * (jnp.arange(ITERS, dtype=F32) + 1.0)
    here = lax.axis_index("space")
    edges = jnp.stack([here > 0, here < space - 1]).astype(F32)
    sig = jnp.concatenate([jnp.sin(phases), jnp.cos(phases), edges])

    vmem = pl.BlockSpec(memory_space=pltpu.VMEM)
    smem = pl.BlockSpec(memory_space=pltpu.SMEM)
    hbm = pl.BlockSpec(memory_space=pltpu.HBM)

    def array(*shape, dtype=F32):
        return jax.ShapeDtypeStruct(shape, dtype)

    held = [
        pltpu.with_memory_space_constraint(a, pltpu.HBM)
        for a in (fwd_current, adj_current, inv_eps)
    ]

    def call(kernel, outs, mib, args, scratch=(), aliases=()):
        return pl.pallas_call(
            kernel,
            out_shape=outs,
            in_specs=[
                smem if a is sig else hbm if any(a is b for b in held) else vmem for a in args
            ],
            out_specs=(vmem,) * len(outs),
            scratch_shapes=scratch,
            input_output_aliases=dict(aliases),
            compiler_params=pltpu.CompilerParams(vmem_limit_bytes=mib * MIB),
        )(*args)

    def traces_for(on_chip):
        (traces,) = call(
            functools.partial(edge_kernel, on_chip),
            (array(E_ROW + 1, ny, nz),),
            4,
            held,
            [
                pltpu.VMEM((2, 3, DEPTH, ny, nz), F32),
                pltpu.VMEM((DEPTH, ny, nz), F32),
                pltpu.SemaphoreType.DMA((3,)),
            ],
        )
        return traces

    from_chip = lax.ppermute(traces_for(True), "space", [(i, i ^ 1) for i in range(space)])
    from_ring = lax.ppermute(
        traces_for(False),
        "space",
        [(i, min(max(i - 1 if i % 2 == 0 else i + 1, 0), space - 1)) for i in range(space)],
    )
    grad, near, mixes, put, pixel = call(
        own_kernel,
        (
            array(groups, planes, width, nz),
            array(2, 8, ny, nz),
            array(2, 2, len(REACHED), 3, ny, nz),
            array(space * 2 * CAP, 4 * count, dtype=BF16),
            array(count, nz, dtype=BF16),
        ),
        20,
        (sig, *held, footprint),
        [
            pltpu.VMEM((3, 2, 3, planes, ny, nz), F32),
            pltpu.VMEM(fwd_current.shape, F32),
            pltpu.VMEM(fwd_current.shape, F32),
            pltpu.VMEM((planes, ny, nz), F32),
            pltpu.SemaphoreType.DMA((3,)),
        ],
    )
    (grad,) = call(
        join_kernel,
        (array(groups, planes, width, nz),),
        16,
        (sig, inv_eps, grad, near, mixes, from_ring, from_chip),
    )
    parts = lax.all_to_all(grad.reshape(groups, count, nz), "src", 0, 0, tiled=True)
    (packed,) = call(pack_kernel, (array(space * 2 * CAP, nz),), 4, (parts, put, pixel))
    arrived = lax.all_to_all(packed.reshape(space, 2 * CAP, nz), "space", 0, 0, tiled=True)
    (sums,) = call(
        pixel_kernel, (array(PIX_DEV, nz),), 4, (arrived.reshape(space * 2 * CAP, nz),)
    )
    return sums


def solution(mesh):
    in_specs = (
        P("src", None, "space", None, None),
        P("src", None, "space", None, None),
        P("space", None, None),
        P("src"),
        P("space", "src"),
    )
    out_specs = P(("src", "space"), None)
    return jax.shard_map(
        per_device, mesh=mesh, in_specs=in_specs, out_specs=out_specs, check_vma=False
    )
```

```python
import functools

import jax
import jax.numpy as jnp
from jax import lax
from jax.experimental import pallas as pl
from jax.experimental.pallas import tpu as pltpu
from jax.sharding import PartitionSpec as P

ITERS = 4
PIX_DEV = 16
CAP = 4
DEPTH = 3
F32 = jnp.float32
BF16 = jnp.bfloat16
MIB = 1024 * 1024


def add(a, b):
    return b if a is None else a if b is None else a + b


def sub(a, b):
    return a if b is None else -b if a is None else a - b


def mul(a, b):
    return None if a is None or b is None else a * b


def y_ahead(a):
    return None if a is None else pltpu.roll(a, a.shape[0] - 1, 0) - a


def y_behind(a):
    return None if a is None else a - pltpu.roll(a, 1, 0)


def z_ahead(a):
    return None if a is None else pltpu.roll(a, a.shape[1] - 1, 1) - a


def z_behind(a):
    return None if a is None else a - pltpu.roll(a, 1, 1)


def curl_f(v, v2_next, v3_next):
    v1, v2, v3 = v
    z1, z2 = z_ahead(v1), z_ahead(v2)
    h2 = sub(z1, sub(v3_next, v3))
    h1 = sub(y_ahead(v3), z2)
    h3 = sub(sub(v2_next, v2), y_ahead(v1))
    return h1, h2, h3


def scaled_curl_b(h, h2_prev, h3_prev, e):
    h1, h2, h3 = h
    z1, z2 = z_behind(h1), z_behind(h2)
    return (
        mul(e, sub(y_behind(h3), z2)),
        mul(e, sub(z1, sub(h3, h3_prev))),
        mul(e, sub(sub(h2, h2_prev), y_behind(h1))),
    )


E_ROW = 12


def trace_row(run, k):
    return 6 * run + 2 * k


def next_is_partner(on_chip):
    return (lax.axis_index("space") % 2 == 0) == on_chip


def edge_kernel(on_chip, fwd_hbm, adj_hbm, eps_hbm, traces, current, eps, sem):
    to_next = next_is_partner(on_chip)
    span = pl.ds(jnp.where(to_next, eps_hbm.shape[0] - DEPTH, 0), DEPTH)
    copies = [(eps_hbm.at[span], eps)]
    for run, whole in enumerate((fwd_hbm, adj_hbm)):
        copies.append((whole.at[0, :, span], current.at[run]))
    copies = [pltpu.make_async_copy(a, b, sem.at[n]) for n, (a, b) in enumerate(copies)]
    for copy in copies:
        copy.start()
    for copy in copies:
        copy.wait()

    def sources():
        e = [-0.25 * eps[i] for i in range(DEPTH)]
        v = [
            [tuple(e[i] * current[run, c, i] for c in range(3)) for i in range(DEPTH)]
            for run in range(2)
        ]
        return e, v

    @pl.when(to_next)
    def _():
        def put(k, plane):
            for run, v in enumerate(plane):
                traces[trace_row(run, k)] = v[2] + z_ahead(v[0])
                traces[trace_row(run, k) + 1] = v[1] + y_ahead(v[0])

        e, v = sources()
        traces[E_ROW] = e[2]
        put(0, [c for _, _, c in v])
        h = [(curl_f(a, b[1], b[2]), curl_f(b, c[1], c[2]), curl_f(c, None, None)) for a, b, c in v]
        v = [
            (scaled_curl_b(hb, ha[1], ha[2], e[1]), scaled_curl_b(hc, hb[1], hb[2], e[2]))
            for ha, hb, hc in h
        ]
        put(1, [c for _, c in v])
        h = [(curl_f(b, c[1], c[2]), curl_f(c, None, None)) for b, c in v]
        put(2, [scaled_curl_b(hc, hb[1], hb[2], e[2]) for hb, hc in h])

    @pl.when(jnp.logical_not(to_next))
    def _():
        def put(k, plane):
            for run, v in enumerate(plane):
                traces[trace_row(run, k)] = v[1]
                traces[trace_row(run, k) + 1] = v[2]

        e, v = sources()
        traces[E_ROW] = e[0]
        put(0, [a for a, _, _ in v])
        h = [(curl_f(a, b[1], b[2]), curl_f(b, c[1], c[2])) for a, b, c in v]
        v = [
            (scaled_curl_b(ha, -a[2], a[1], e[0]), scaled_curl_b(hb, ha[1], ha[2], e[1]))
            for (ha, hb), (a, _, _) in zip(h, v)
        ]
        put(1, [a for a, _ in v])
        h = [curl_f(a, b[1], b[2]) for a, b in v]
        put(2, [scaled_curl_b(ha, -a[2], a[1], e[0]) for ha, (a, _) in zip(h, v)])


def pair_factors(sig):
    def by_step(s):
        s1, s2, s3, s4 = s
        return (
            (s1,),
            (s1 + s2, s1),
            (s1 + s2 + s3, 3.0 * s1 + s2, s1),
            (s1 + s2 + s3 + s4, 6.0 * s1 + 3.0 * s2 + s3, 5.0 * s1 + s2, s1),
        )

    f = by_step([sig[i] for i in range(ITERS)])
    a = by_step([sig[ITERS + i] for i in range(ITERS)])
    factors = {}
    for t in range(ITERS):
        for k, fk in enumerate(f[t]):
            for m, am in enumerate(a[ITERS - 1 - t]):
                factors[k, m] = factors.get((k, m), 0.0) + 4.0 * fk * am
    return factors


REACHED = tuple((depth, k) for depth in range(DEPTH) for k in range(depth + 1, DEPTH + 1))


def own_kernel(
    sig, fwd_hbm, adj_hbm, eps_hbm, footprint, out, near, mixes, put, pixel, v, fwd, adj, eps, sem
):
    pairs = ((fwd_hbm, fwd), (adj_hbm, adj), (eps_hbm, eps))
    copies = [pltpu.make_async_copy(a, b, sem.at[n]) for n, (a, b) in enumerate(pairs)]
    for copy in copies:
        copy.start()
    for copy in copies:
        copy.wait()
    planes = eps.shape[0]
    last = planes - 1
    has_prev = sig[8]
    factors = pair_factors(sig)

    def start(i, _):
        e = -0.25 * eps[i]
        for run, current in enumerate((fwd, adj)):
            for c in range(3):
                v[0, run, c, i] = e * current[0, c, i]
        return 0

    lax.fori_loop(0, planes, start, 0)

    def read(k, run, i):
        return tuple(v[k, run, c, i] for c in range(3))

    for k in range(DEPTH):
        behind = []
        for run in range(2):
            if k < 2:
                near[run, 2 * k] = v[k, run, 1, 0]
                near[run, 2 * k + 1] = v[k, run, 2, 0]
            behind += [v[k, run, 2, 0] * -has_prev, v[k, run, 1, 0] * has_prev]

        def finish(i, new):
            if k < 2:
                for run in range(2):
                    for c in range(3):
                        v[k + 1, run, c, i] = new[run][c]
                return
            total = None
            for c in range(3):
                f = [v[j, 0, c, i] for j in range(DEPTH)] + [new[0][c]]
                a = [v[j, 1, c, i] for j in range(DEPTH)] + [new[1][c]]
                for m in range(4):
                    mix = None
                    for j in range(4 - m):
                        mix = add(mix, factors[j, m] * f[j])
                    total = add(total, mix * a[m])
            for block in range(out.shape[0]):
                out[block, i] = total[block * 8 : block * 8 + 8]

        def plane(i, carry):
            e = -0.25 * eps[i]
            h = [curl_f(read(k, r, i), v[k, r, 1, i + 1], v[k, r, 2, i + 1]) for r in range(2)]
            finish(i, [scaled_curl_b(h[r], carry[2 * r], carry[2 * r + 1], e) for r in range(2)])
            return h[0][1], h[0][2], h[1][1], h[1][2]

        carry = lax.fori_loop(0, last, plane, tuple(behind))
        new = []
        for run in range(2):
            h = curl_f(read(k, run, last), None, None)
            if k < 2:
                near[run, 4 + 2 * k] = h[1]
                near[run, 5 + 2 * k] = h[2]
            new.append(scaled_curl_b(h, carry[2 * run], carry[2 * run + 1], -0.25 * eps[last]))
        finish(last, new)

    for side in range(2):
        for n, (depth, k) in enumerate(REACHED):
            i = last - depth if side else depth
            for c in range(3):
                for run in range(2):
                    mix = None
                    for j in range(4 - k):
                        factor = factors[(j, k) if run else (k, j)]
                        mix = add(mix, factor * v[j, 1 - run, c, i])
                    mixes[side, run, n, c] = mix

    wide, width = footprint.shape
    count = wide * width
    owners = put.shape[0] // (2 * CAP)
    ids = footprint[...]
    by_row = jnp.concatenate(
        [jnp.broadcast_to(ids[i : i + 1], (width, width)) for i in range(wide)], axis=0
    ).astype(F32)
    at = lax.broadcasted_iota(jnp.int32, (count, width), 0) % width
    own = at == lax.broadcasted_iota(jnp.int32, (count, width), 1)
    col = jnp.sum(jnp.where(own, by_row, 0.0), axis=1, keepdims=True)
    diagonal = lax.broadcasted_iota(jnp.int32, (count, count), 0) == lax.broadcasted_iota(
        jnp.int32, (count, count), 1
    )
    row = jnp.sum(jnp.where(diagonal, col, 0.0), axis=0, keepdims=True)
    row, col = row.astype(jnp.int32), col.astype(jnp.int32)
    lanes = lax.broadcasted_iota(jnp.int32, pixel.shape, 1)
    pixel[...] = ((col & (PIX_DEV - 1)) == lanes).astype(F32).astype(BF16)
    row_owner = (row >> 4) & (owners - 1)
    col_owner = (col >> 4) & (owners - 1)
    earlier = lax.broadcasted_iota(jnp.int32, (count, count), 0) < lax.broadcasted_iota(
        jnp.int32, (count, count), 1
    )
    same = (row_owner == col_owner) & earlier
    rank = jnp.sum(same.astype(F32), axis=0, keepdims=True).astype(jnp.int32)
    slot = row_owner * (2 * CAP) + rank
    rows = lax.broadcasted_iota(jnp.int32, (put.shape[0], count), 0)
    value = (rows == slot).astype(F32)
    mark = (rows == slot + CAP).astype(F32)
    put[...] = jnp.concatenate([value, value, value, mark], axis=1).astype(BF16)


def join_kernel(sig, eps, grad, near, mixes, from_ring, from_chip, out):
    last = eps.shape[0] - 1
    has_prev, has_next = sig[8], sig[9]
    runs = range(2)
    first_of_pair = lax.axis_index("space") % 2 == 0

    def from_prev(row):
        return jnp.where(first_of_pair, from_ring[row], from_chip[row])

    def from_next(row):
        return jnp.where(first_of_pair, from_chip[row], from_ring[row])

    e_prev, e_next = from_prev(E_ROW) * has_prev, from_next(E_ROW) * has_next
    e = {i: -0.25 * eps[i] for i in (0, 1, 2, last - 2, last - 1, last)}
    factors = pair_factors(sig)

    def left_trace(r, k):
        row = trace_row(r, k)
        return from_prev(row) * has_prev, from_prev(row + 1) * -has_prev

    def right_trace(r, k):
        row = trace_row(r, k)
        return from_next(row + 1) * -has_next, from_next(row) * has_next

    def passed(h, e):
        return None, e * h[1], -e * h[0]

    t = [left_trace(r, 0) for r in runs]
    u = [right_trace(r, 0) for r in runs]
    own = [(None, -near[r, 1], near[r, 0]) for r in runs]
    c = [scaled_curl_b(own[r], None, None, e_prev) for r in runs]
    g1 = [scaled_curl_b((None, *u[r]), None, None, e[last]) for r in runs]
    f1 = [passed(t[r], e[0]) for r in runs]
    d = [passed((near[r, 4], near[r, 5]), e_next) for r in runs]
    h0 = [curl_f(f1[r], None, None) for r in runs]
    hm = [curl_f(c[r], f1[r][1], f1[r][2]) for r in runs]
    hd = [curl_f(d[r], None, None) for r in runs]
    h7 = [curl_f(g1[r], d[r][1], d[r][2]) for r in runs]
    h6 = [(-g1[r][2], g1[r][1]) for r in runs]
    t = [left_trace(r, 1) for r in runs]
    u = [right_trace(r, 1) for r in runs]
    f2a = [scaled_curl_b(h0[r], hm[r][1] + t[r][0], hm[r][2] + t[r][1], e[0]) for r in runs]
    c = [
        scaled_curl_b(
            (hm[r][0], hm[r][1] - near[r, 3], hm[r][2] + near[r, 2]), -c[r][2], c[r][1], e_prev
        )
        for r in runs
    ]
    f2b = [passed(h0[r][1:], e[1]) for r in runs]
    g2a = [
        scaled_curl_b((h7[r][0], h7[r][1] + u[r][0], h7[r][2] + u[r][1]), *h6[r], e[last])
        for r in runs
    ]
    g2b = [scaled_curl_b((None, *h6[r]), None, None, e[last - 1]) for r in runs]
    d = [
        scaled_curl_b(hd[r], near[r, 6] + h7[r][1], near[r, 7] + h7[r][2], e_next) for r in runs
    ]
    h0 = [curl_f(f2a[r], f2b[r][1], f2b[r][2]) for r in runs]
    h1 = [curl_f(f2b[r], None, None) for r in runs]
    hm = [curl_f(c[r], f2a[r][1], f2a[r][2]) for r in runs]
    h7 = [curl_f(g2a[r], d[r][1], d[r][2]) for r in runs]
    h6 = [curl_f(g2b[r], g2a[r][1], g2a[r][2]) for r in runs]
    h5 = [(-g2b[r][2], g2b[r][1]) for r in runs]
    t = [left_trace(r, 2) for r in runs]
    u = [right_trace(r, 2) for r in runs]
    f3a = [scaled_curl_b(h0[r], hm[r][1] + t[r][0], hm[r][2] + t[r][1], e[0]) for r in runs]
    f3b = [scaled_curl_b(h1[r], h0[r][1], h0[r][2], e[1]) for r in runs]
    f3c = [passed(h1[r][1:], e[2]) for r in runs]
    g3a = [
        scaled_curl_b(
            (h7[r][0], h7[r][1] + u[r][0], h7[r][2] + u[r][1]), h6[r][1], h6[r][2], e[last]
        )
        for r in runs
    ]
    g3b = [scaled_curl_b(h6[r], *h5[r], e[last - 1]) for r in runs]
    g3c = [scaled_curl_b((None, *h5[r]), None, None, e[last - 2]) for r in runs]

    fields = (
        ({(0, 1): f1, (0, 2): f2a, (0, 3): f3a, (1, 2): f2b, (1, 3): f3b, (2, 3): f3c}),
        ({(0, 1): g1, (0, 2): g2a, (0, 3): g3a, (1, 2): g2b, (1, 3): g3b, (2, 3): g3c}),
    )
    for i in range(DEPTH, last + 1 - DEPTH):
        for block in range(out.shape[0]):
            out[block, i] = grad[block, i]
    for side in range(2):
        for depth in range(DEPTH):
            i = last - depth if side else depth
            total = None
            for n, (at, k) in enumerate(REACHED):
                if at == depth:
                    f = fields[side][at, k]
                    for x in range(3):
                        for r in runs:
                            if f[r][x] is not None:
                                total = add(total, f[r][x] * mixes[side, r, n, x])
            if depth == 0:
                one, two = fields[side][0, 1], fields[side][0, 2]
                for x in range(3):
                    if one[0][x] is not None:
                        both = factors[1, 1] * one[1][x] + factors[1, 2] * two[1][x]
                        total = total + one[0][x] * both
                        total = total + two[0][x] * (factors[2, 1] * one[1][x])
            for block in range(out.shape[0]):
                out[block, i] = grad[block, i] + total[block * 8 : block * 8 + 8]


def in_thirds(a):
    high = a.astype(BF16)
    rest = a - high.astype(F32)
    middle = rest.astype(BF16)
    return high, middle, (rest - middle.astype(F32)).astype(BF16)


def pack_kernel(parts, put, pixel, out):
    summed = parts[0]
    for s in range(1, parts.shape[0]):
        summed = summed + parts[s]
    rows = jnp.concatenate([*in_thirds(summed), pixel[...]], axis=0)
    out[...] = jnp.dot(put[...], rows, preferred_element_type=F32)


def pixel_kernel(arrived, out):
    got = arrived[...]
    rows = lax.broadcasted_iota(jnp.int32, got.shape, 0)
    is_data = (rows & (2 * CAP - 1)) < CAP
    pixel = jnp.where(is_data, pltpu.roll(got, got.shape[0] - CAP, 0), 0.0).astype(BF16)
    sums = None
    for part in in_thirds(got):
        sums = add(
            sums,
            lax.dot_general(pixel, part, (((0,), (0,)), ((), ())), preferred_element_type=F32),
        )
    out[...] = sums[: out.shape[0]]


def per_device(fwd_current, adj_current, inv_eps, wavelength, footprint):
    planes, ny, nz = inv_eps.shape
    space = lax.axis_size("space")
    groups = lax.axis_size("src")
    width = ny // groups
    count = planes * width
    omega = 0.25 + 0.05 * wavelength.astype(F32)
    phases = omega * (jnp.arange(ITERS, dtype=F32) + 1.0)
    here = lax.axis_index("space")
    edges = jnp.stack([here > 0, here < space - 1]).astype(F32)
    sig = jnp.concatenate([jnp.sin(phases), jnp.cos(phases), edges])

    vmem = pl.BlockSpec(memory_space=pltpu.VMEM)
    smem = pl.BlockSpec(memory_space=pltpu.SMEM)
    hbm = pl.BlockSpec(memory_space=pltpu.HBM)

    def array(*shape, dtype=F32):
        return jax.ShapeDtypeStruct(shape, dtype)

    held = [
        pltpu.with_memory_space_constraint(a, pltpu.HBM)
        for a in (fwd_current, adj_current, inv_eps)
    ]

    def call(kernel, outs, mib, args, scratch=(), aliases=()):
        return pl.pallas_call(
            kernel,
            out_shape=outs,
            in_specs=[
                smem if a is sig else hbm if any(a is b for b in held) else vmem for a in args
            ],
            out_specs=(vmem,) * len(outs),
            scratch_shapes=scratch,
            input_output_aliases=dict(aliases),
            compiler_params=pltpu.CompilerParams(vmem_limit_bytes=mib * MIB),
        )(*args)

    def traces_for(on_chip):
        (traces,) = call(
            functools.partial(edge_kernel, on_chip),
            (array(E_ROW + 1, ny, nz),),
            4,
            held,
            [
                pltpu.VMEM((2, 3, DEPTH, ny, nz), F32),
                pltpu.VMEM((DEPTH, ny, nz), F32),
                pltpu.SemaphoreType.DMA((3,)),
            ],
        )
        return traces

    from_chip = lax.ppermute(traces_for(True), "space", [(i, i ^ 1) for i in range(space)])
    from_ring = lax.ppermute(
        traces_for(False),
        "space",
        [(i, (i - 1 if i % 2 == 0 else i + 1) % space) for i in range(space)],
    )
    grad, near, mixes, put, pixel = call(
        own_kernel,
        (
            array(groups, planes, width, nz),
            array(2, 8, ny, nz),
            array(2, 2, len(REACHED), 3, ny, nz),
            array(space * 2 * CAP, 4 * count, dtype=BF16),
            array(count, nz, dtype=BF16),
        ),
        20,
        (sig, *held, footprint),
        [
            pltpu.VMEM((3, 2, 3, planes, ny, nz), F32),
            pltpu.VMEM(fwd_current.shape, F32),
            pltpu.VMEM(fwd_current.shape, F32),
            pltpu.VMEM((planes, ny, nz), F32),
            pltpu.SemaphoreType.DMA((3,)),
        ],
    )
    (grad,) = call(
        join_kernel,
        (array(groups, planes, width, nz),),
        16,
        (sig, inv_eps, grad, near, mixes, from_ring, from_chip),
    )
    parts = lax.all_to_all(grad.reshape(groups, count, nz), "src", 0, 0, tiled=True)
    (packed,) = call(pack_kernel, (array(space * 2 * CAP, nz),), 4, (parts, put, pixel))
    arrived = lax.all_to_all(packed.reshape(space, 2 * CAP, nz), "space", 0, 0, tiled=True)
    (sums,) = call(
        pixel_kernel, (array(PIX_DEV, nz),), 4, (arrived.reshape(space * 2 * CAP, nz),)
    )
    return sums


def solution(mesh):
    in_specs = (
        P("src", None, "space", None, None),
        P("src", None, "space", None, None),
        P("space", None, None),
        P("src"),
        P("space", "src"),
    )
    out_specs = P(("src", "space"), None)
    return jax.shard_map(
        per_device, mesh=mesh, in_specs=in_specs, out_specs=out_specs, check_vma=False
    )
```

```python
import functools

import jax
import jax.numpy as jnp
from jax import lax
from jax.experimental import pallas as pl
from jax.experimental.pallas import tpu as pltpu
from jax.sharding import PartitionSpec as P

ITERS = 4
PIX_DEV = 16
CAP = 4
DEPTH = 3
F32 = jnp.float32
BF16 = jnp.bfloat16
MIB = 1024 * 1024


def add(a, b):
    return b if a is None else a if b is None else a + b


def sub(a, b):
    return a if b is None else -b if a is None else a - b


def mul(a, b):
    return None if a is None or b is None else a * b


def y_ahead(a):
    return None if a is None else pltpu.roll(a, a.shape[0] - 1, 0) - a


def y_behind(a):
    return None if a is None else a - pltpu.roll(a, 1, 0)


def z_ahead(a):
    return None if a is None else pltpu.roll(a, a.shape[1] - 1, 1) - a


def z_behind(a):
    return None if a is None else a - pltpu.roll(a, 1, 1)


def curl_f(v, v2_next, v3_next):
    v1, v2, v3 = v
    z1, z2 = z_ahead(v1), z_ahead(v2)
    h2 = sub(z1, sub(v3_next, v3))
    h1 = sub(y_ahead(v3), z2)
    h3 = sub(sub(v2_next, v2), y_ahead(v1))
    return h1, h2, h3


def scaled_curl_b(h, h2_prev, h3_prev, e):
    h1, h2, h3 = h
    z1, z2 = z_behind(h1), z_behind(h2)
    return (
        mul(e, sub(y_behind(h3), z2)),
        mul(e, sub(z1, sub(h3, h3_prev))),
        mul(e, sub(sub(h2, h2_prev), y_behind(h1))),
    )


E_ROW = 12


def trace_row(run, k):
    return 6 * run + 2 * k


def next_is_partner(on_chip):
    return (lax.axis_index("space") % 2 == 0) == on_chip


def edge_kernel(on_chip, fwd_hbm, adj_hbm, eps_hbm, traces, current, eps, sem):
    to_next = next_is_partner(on_chip)
    span = pl.ds(jnp.where(to_next, eps_hbm.shape[0] - DEPTH, 0), DEPTH)
    copies = [(eps_hbm.at[span], eps)]
    for run, whole in enumerate((fwd_hbm, adj_hbm)):
        copies.append((whole.at[0, :, span], current.at[run]))
    copies = [pltpu.make_async_copy(a, b, sem.at[n]) for n, (a, b) in enumerate(copies)]
    for copy in copies:
        copy.start()
    for copy in copies:
        copy.wait()

    def sources():
        e = [-0.25 * eps[i] for i in range(DEPTH)]
        v = [
            [tuple(e[i] * current[run, c, i] for c in range(3)) for i in range(DEPTH)]
            for run in range(2)
        ]
        return e, v

    @pl.when(to_next)
    def _():
        def put(k, plane):
            for run, v in enumerate(plane):
                traces[trace_row(run, k)] = v[2] + z_ahead(v[0])
                traces[trace_row(run, k) + 1] = v[1] + y_ahead(v[0])

        e, v = sources()
        traces[E_ROW] = e[2]
        put(0, [c for _, _, c in v])
        h = [(curl_f(a, b[1], b[2]), curl_f(b, c[1], c[2]), curl_f(c, None, None)) for a, b, c in v]
        v = [
            (scaled_curl_b(hb, ha[1], ha[2], e[1]), scaled_curl_b(hc, hb[1], hb[2], e[2]))
            for ha, hb, hc in h
        ]
        put(1, [c for _, c in v])
        h = [(curl_f(b, c[1], c[2]), curl_f(c, None, None)) for b, c in v]
        put(2, [scaled_curl_b(hc, hb[1], hb[2], e[2]) for hb, hc in h])

    @pl.when(jnp.logical_not(to_next))
    def _():
        def put(k, plane):
            for run, v in enumerate(plane):
                traces[trace_row(run, k)] = v[1]
                traces[trace_row(run, k) + 1] = v[2]

        e, v = sources()
        traces[E_ROW] = e[0]
        put(0, [a for a, _, _ in v])
        h = [(curl_f(a, b[1], b[2]), curl_f(b, c[1], c[2])) for a, b, c in v]
        v = [
            (scaled_curl_b(ha, -a[2], a[1], e[0]), scaled_curl_b(hb, ha[1], ha[2], e[1]))
            for (ha, hb), (a, _, _) in zip(h, v)
        ]
        put(1, [a for a, _ in v])
        h = [curl_f(a, b[1], b[2]) for a, b in v]
        put(2, [scaled_curl_b(ha, -a[2], a[1], e[0]) for ha, (a, _) in zip(h, v)])


def pair_factors(sig):
    def by_step(s):
        s1, s2, s3, s4 = s
        return (
            (s1,),
            (s1 + s2, s1),
            (s1 + s2 + s3, 3.0 * s1 + s2, s1),
            (s1 + s2 + s3 + s4, 6.0 * s1 + 3.0 * s2 + s3, 5.0 * s1 + s2, s1),
        )

    f = by_step([sig[i] for i in range(ITERS)])
    a = by_step([sig[ITERS + i] for i in range(ITERS)])
    factors = {}
    for t in range(ITERS):
        for k, fk in enumerate(f[t]):
            for m, am in enumerate(a[ITERS - 1 - t]):
                factors[k, m] = factors.get((k, m), 0.0) + 4.0 * fk * am
    return factors


REACHED = tuple((depth, k) for depth in range(DEPTH) for k in range(depth + 1, DEPTH + 1))


def own_kernel(
    sig, fwd_hbm, adj_hbm, eps_hbm, footprint, out, near, mixes, put, pixel, v, fwd, adj, eps, sem
):
    pairs = ((fwd_hbm, fwd), (adj_hbm, adj), (eps_hbm, eps))
    copies = [pltpu.make_async_copy(a, b, sem.at[n]) for n, (a, b) in enumerate(pairs)]
    for copy in copies:
        copy.start()
    for copy in copies:
        copy.wait()
    planes = eps.shape[0]
    last = planes - 1
    has_prev = sig[8]
    factors = pair_factors(sig)

    def start(i, _):
        e = -0.25 * eps[i]
        for run, current in enumerate((fwd, adj)):
            for c in range(3):
                v[0, run, c, i] = e * current[0, c, i]
        return 0

    lax.fori_loop(0, planes, start, 0)

    def read(k, run, i):
        return tuple(v[k, run, c, i] for c in range(3))

    for k in range(DEPTH):
        behind = []
        for run in range(2):
            if k < 2:
                near[run, 2 * k] = v[k, run, 1, 0]
                near[run, 2 * k + 1] = v[k, run, 2, 0]
            behind += [v[k, run, 2, 0] * -has_prev, v[k, run, 1, 0] * has_prev]

        def finish(i, new):
            if k < 2:
                for run in range(2):
                    for c in range(3):
                        v[k + 1, run, c, i] = new[run][c]
                return
            total = None
            for c in range(3):
                f = [v[j, 0, c, i] for j in range(DEPTH)] + [new[0][c]]
                a = [v[j, 1, c, i] for j in range(DEPTH)] + [new[1][c]]
                for m in range(4):
                    mix = None
                    for j in range(4 - m):
                        mix = add(mix, factors[j, m] * f[j])
                    total = add(total, mix * a[m])
            for block in range(out.shape[0]):
                out[block, i] = total[block * 8 : block * 8 + 8]

        def plane(i, carry):
            e = -0.25 * eps[i]
            h = [curl_f(read(k, r, i), v[k, r, 1, i + 1], v[k, r, 2, i + 1]) for r in range(2)]
            finish(i, [scaled_curl_b(h[r], carry[2 * r], carry[2 * r + 1], e) for r in range(2)])
            return h[0][1], h[0][2], h[1][1], h[1][2]

        carry = lax.fori_loop(0, last, plane, tuple(behind))
        new = []
        for run in range(2):
            h = curl_f(read(k, run, last), None, None)
            if k < 2:
                near[run, 4 + 2 * k] = h[1]
                near[run, 5 + 2 * k] = h[2]
            new.append(scaled_curl_b(h, carry[2 * run], carry[2 * run + 1], -0.25 * eps[last]))
        finish(last, new)

    for side in range(2):
        for n, (depth, k) in enumerate(REACHED):
            i = last - depth if side else depth
            for c in range(3):
                for run in range(2):
                    mix = None
                    for j in range(4 - k):
                        factor = factors[(j, k) if run else (k, j)]
                        mix = add(mix, factor * v[j, 1 - run, c, i])
                    mixes[side, run, n, c] = mix

    wide, width = footprint.shape
    count = wide * width
    owners = put.shape[0] // (CAP + 1)
    ids = footprint[...]
    by_row = jnp.concatenate(
        [jnp.broadcast_to(ids[i : i + 1], (width, width)) for i in range(wide)], axis=0
    ).astype(F32)
    at = lax.broadcasted_iota(jnp.int32, (count, width), 0) % width
    own = at == lax.broadcasted_iota(jnp.int32, (count, width), 1)
    col = jnp.sum(jnp.where(own, by_row, 0.0), axis=1, keepdims=True)
    diagonal = lax.broadcasted_iota(jnp.int32, (count, count), 0) == lax.broadcasted_iota(
        jnp.int32, (count, count), 1
    )
    row = jnp.sum(jnp.where(diagonal, col, 0.0), axis=0, keepdims=True)
    row, col = row.astype(jnp.int32), col.astype(jnp.int32)
    row_owner = (row >> 4) & (owners - 1)
    col_owner = (col >> 4) & (owners - 1)
    one, two = (lax.broadcasted_iota(jnp.int32, (count, count), axis) for axis in range(2))
    same = (row_owner == col_owner).astype(F32)
    row_rank = jnp.sum(jnp.where(one < two, same, 0.0), axis=0, keepdims=True).astype(jnp.int32)
    col_rank = jnp.sum(jnp.where(two < one, same, 0.0), axis=1, keepdims=True).astype(jnp.int32)
    lanes = lax.broadcasted_iota(jnp.int32, pixel.shape, 1)
    pixel[...] = ((col & (PIX_DEV - 1)) + col_rank * PIX_DEV == lanes).astype(F32).astype(BF16)
    rows = lax.broadcasted_iota(jnp.int32, (put.shape[0], count), 0)
    value = (rows == row_rank * owners + row_owner).astype(F32)
    mark = (rows == CAP * owners + row_owner).astype(F32)
    put[...] = jnp.concatenate([value, value, value, mark], axis=1).astype(BF16)


def join_kernel(sig, eps, grad, near, mixes, from_ring, from_chip, out):
    last = eps.shape[0] - 1
    has_prev, has_next = sig[8], sig[9]
    runs = range(2)
    first_of_pair = lax.axis_index("space") % 2 == 0

    def from_prev(row):
        return jnp.where(first_of_pair, from_ring[row], from_chip[row])

    def from_next(row):
        return jnp.where(first_of_pair, from_chip[row], from_ring[row])

    e_prev, e_next = from_prev(E_ROW) * has_prev, from_next(E_ROW) * has_next
    e = {i: -0.25 * eps[i] for i in (0, 1, 2, last - 2, last - 1, last)}
    factors = pair_factors(sig)

    def left_trace(r, k):
        row = trace_row(r, k)
        return from_prev(row) * has_prev, from_prev(row + 1) * -has_prev

    def right_trace(r, k):
        row = trace_row(r, k)
        return from_next(row + 1) * -has_next, from_next(row) * has_next

    def passed(h, e):
        return None, e * h[1], -e * h[0]

    t = [left_trace(r, 0) for r in runs]
    u = [right_trace(r, 0) for r in runs]
    own = [(None, -near[r, 1], near[r, 0]) for r in runs]
    c = [scaled_curl_b(own[r], None, None, e_prev) for r in runs]
    g1 = [scaled_curl_b((None, *u[r]), None, None, e[last]) for r in runs]
    f1 = [passed(t[r], e[0]) for r in runs]
    d = [passed((near[r, 4], near[r, 5]), e_next) for r in runs]
    h0 = [curl_f(f1[r], None, None) for r in runs]
    hm = [curl_f(c[r], f1[r][1], f1[r][2]) for r in runs]
    hd = [curl_f(d[r], None, None) for r in runs]
    h7 = [curl_f(g1[r], d[r][1], d[r][2]) for r in runs]
    h6 = [(-g1[r][2], g1[r][1]) for r in runs]
    t = [left_trace(r, 1) for r in runs]
    u = [right_trace(r, 1) for r in runs]
    f2a = [scaled_curl_b(h0[r], hm[r][1] + t[r][0], hm[r][2] + t[r][1], e[0]) for r in runs]
    c = [
        scaled_curl_b(
            (hm[r][0], hm[r][1] - near[r, 3], hm[r][2] + near[r, 2]), -c[r][2], c[r][1], e_prev
        )
        for r in runs
    ]
    f2b = [passed(h0[r][1:], e[1]) for r in runs]
    g2a = [
        scaled_curl_b((h7[r][0], h7[r][1] + u[r][0], h7[r][2] + u[r][1]), *h6[r], e[last])
        for r in runs
    ]
    g2b = [scaled_curl_b((None, *h6[r]), None, None, e[last - 1]) for r in runs]
    d = [
        scaled_curl_b(hd[r], near[r, 6] + h7[r][1], near[r, 7] + h7[r][2], e_next) for r in runs
    ]
    h0 = [curl_f(f2a[r], f2b[r][1], f2b[r][2]) for r in runs]
    h1 = [curl_f(f2b[r], None, None) for r in runs]
    hm = [curl_f(c[r], f2a[r][1], f2a[r][2]) for r in runs]
    h7 = [curl_f(g2a[r], d[r][1], d[r][2]) for r in runs]
    h6 = [curl_f(g2b[r], g2a[r][1], g2a[r][2]) for r in runs]
    h5 = [(-g2b[r][2], g2b[r][1]) for r in runs]
    t = [left_trace(r, 2) for r in runs]
    u = [right_trace(r, 2) for r in runs]
    f3a = [scaled_curl_b(h0[r], hm[r][1] + t[r][0], hm[r][2] + t[r][1], e[0]) for r in runs]
    f3b = [scaled_curl_b(h1[r], h0[r][1], h0[r][2], e[1]) for r in runs]
    f3c = [passed(h1[r][1:], e[2]) for r in runs]
    g3a = [
        scaled_curl_b(
            (h7[r][0], h7[r][1] + u[r][0], h7[r][2] + u[r][1]), h6[r][1], h6[r][2], e[last]
        )
        for r in runs
    ]
    g3b = [scaled_curl_b(h6[r], *h5[r], e[last - 1]) for r in runs]
    g3c = [scaled_curl_b((None, *h5[r]), None, None, e[last - 2]) for r in runs]

    fields = (
        ({(0, 1): f1, (0, 2): f2a, (0, 3): f3a, (1, 2): f2b, (1, 3): f3b, (2, 3): f3c}),
        ({(0, 1): g1, (0, 2): g2a, (0, 3): g3a, (1, 2): g2b, (1, 3): g3b, (2, 3): g3c}),
    )
    for i in range(DEPTH, last + 1 - DEPTH):
        for block in range(out.shape[0]):
            out[block, i] = grad[block, i]
    for side in range(2):
        for depth in range(DEPTH):
            i = last - depth if side else depth
            total = None
            for n, (at, k) in enumerate(REACHED):
                if at == depth:
                    f = fields[side][at, k]
                    for x in range(3):
                        for r in runs:
                            if f[r][x] is not None:
                                total = add(total, f[r][x] * mixes[side, r, n, x])
            if depth == 0:
                one, two = fields[side][0, 1], fields[side][0, 2]
                for x in range(3):
                    if one[0][x] is not None:
                        both = factors[1, 1] * one[1][x] + factors[1, 2] * two[1][x]
                        total = total + one[0][x] * both
                        total = total + two[0][x] * (factors[2, 1] * one[1][x])
            for block in range(out.shape[0]):
                out[block, i] = grad[block, i] + total[block * 8 : block * 8 + 8]


def in_thirds(a):
    high = a.astype(BF16)
    rest = a - high.astype(F32)
    middle = rest.astype(BF16)
    return high, middle, (rest - middle.astype(F32)).astype(BF16)


def pack_kernel(parts, put, pixel, out):
    summed = parts[0]
    for s in range(1, parts.shape[0]):
        summed = summed + parts[s]
    rows = jnp.concatenate([*in_thirds(summed), pixel[...]], axis=0)
    packed = jnp.dot(put[...], rows, preferred_element_type=F32)
    owners, _, width = out.shape
    depth = width // (CAP + 1)
    for j in range(CAP + 1):
        out[:, 0, j * depth : (j + 1) * depth] = packed[j * owners : (j + 1) * owners]


def pixel_kernel(arrived, out):
    depth = out.shape[1]
    marks = arrived[:, 0, CAP * depth :]
    pixel = jnp.concatenate(
        [marks] + [pltpu.roll(marks, depth - j * PIX_DEV, 1) for j in range(1, CAP)], axis=0
    ).astype(BF16)
    got = jnp.concatenate(
        [arrived[:, 0, j * depth : (j + 1) * depth] for j in range(CAP)], axis=0
    )
    sums = None
    for part in in_thirds(got):
        sums = add(
            sums,
            lax.dot_general(pixel, part, (((0,), (0,)), ((), ())), preferred_element_type=F32),
        )
    out[...] = sums[: out.shape[0]]


def per_device(fwd_current, adj_current, inv_eps, wavelength, footprint):
    planes, ny, nz = inv_eps.shape
    space = lax.axis_size("space")
    groups = lax.axis_size("src")
    width = ny // groups
    count = planes * width
    omega = 0.25 + 0.05 * wavelength.astype(F32)
    phases = omega * (jnp.arange(ITERS, dtype=F32) + 1.0)
    here = lax.axis_index("space")
    edges = jnp.stack([here > 0, here < space - 1]).astype(F32)
    sig = jnp.concatenate([jnp.sin(phases), jnp.cos(phases), edges])

    vmem = pl.BlockSpec(memory_space=pltpu.VMEM)
    smem = pl.BlockSpec(memory_space=pltpu.SMEM)
    hbm = pl.BlockSpec(memory_space=pltpu.HBM)

    def array(*shape, dtype=F32):
        return jax.ShapeDtypeStruct(shape, dtype)

    held = [
        pltpu.with_memory_space_constraint(a, pltpu.HBM)
        for a in (fwd_current, adj_current, inv_eps)
    ]

    def call(kernel, outs, mib, args, scratch=(), aliases=()):
        return pl.pallas_call(
            kernel,
            out_shape=outs,
            in_specs=[
                smem if a is sig else hbm if any(a is b for b in held) else vmem for a in args
            ],
            out_specs=(vmem,) * len(outs),
            scratch_shapes=scratch,
            input_output_aliases=dict(aliases),
            compiler_params=pltpu.CompilerParams(vmem_limit_bytes=mib * MIB),
        )(*args)

    def traces_for(on_chip):
        (traces,) = call(
            functools.partial(edge_kernel, on_chip),
            (array(E_ROW + 1, ny, nz),),
            4,
            held,
            [
                pltpu.VMEM((2, 3, DEPTH, ny, nz), F32),
                pltpu.VMEM((DEPTH, ny, nz), F32),
                pltpu.SemaphoreType.DMA((3,)),
            ],
        )
        return traces

    from_chip = lax.ppermute(traces_for(True), "space", [(i, i ^ 1) for i in range(space)])
    from_ring = lax.ppermute(
        traces_for(False),
        "space",
        [(i, (i - 1 if i % 2 == 0 else i + 1) % space) for i in range(space)],
    )
    grad, near, mixes, put, pixel = call(
        own_kernel,
        (
            array(groups, planes, width, nz),
            array(2, 8, ny, nz),
            array(2, 2, len(REACHED), 3, ny, nz),
            array(space * (CAP + 1), 4 * count, dtype=BF16),
            array(count, nz, dtype=BF16),
        ),
        20,
        (sig, *held, footprint),
        [
            pltpu.VMEM((3, 2, 3, planes, ny, nz), F32),
            pltpu.VMEM(fwd_current.shape, F32),
            pltpu.VMEM(fwd_current.shape, F32),
            pltpu.VMEM((planes, ny, nz), F32),
            pltpu.SemaphoreType.DMA((3,)),
        ],
    )
    (grad,) = call(
        join_kernel,
        (array(groups, planes, width, nz),),
        16,
        (sig, inv_eps, grad, near, mixes, from_ring, from_chip),
    )
    parts = lax.all_to_all(grad.reshape(groups, count, nz), "src", 0, 0, tiled=True)
    (packed,) = call(
        pack_kernel, (array(space, 1, (CAP + 1) * nz),), 4, (parts, put, pixel)
    )
    arrived = lax.all_to_all(packed, "space", 0, 0, tiled=True)
    (sums,) = call(pixel_kernel, (array(PIX_DEV, nz),), 4, (arrived,))
    return sums


def solution(mesh):
    in_specs = (
        P("src", None, "space", None, None),
        P("src", None, "space", None, None),
        P("space", None, None),
        P("src"),
        P("space", "src"),
    )
    out_specs = P(("src", "space"), None)
    return jax.shard_map(
        per_device, mesh=mesh, in_specs=in_specs, out_specs=out_specs, check_vma=False
    )
```
